128 devices in a mesh: pts: 16 (over x, z), nbr: 8 (over y, core).
Axes of the slice: x: 4, y: 4, z: 4, core: 2. Of those that a mesh axis runs over, the one named last changes fastest.
Arguments:
- points: bfloat16 [16, 8, 4096, 128], P('pts', 'nbr'), may hold values from -6 to 6
- dest_owner: int32 [16, 8, 4096, 1], P('pts', 'nbr'), may hold values from 0 to 127; in each aligned block of 4096 rows (0 to 4095, 4096 to 8191, ..., all dimensions but the last counted through in order) at most 64 rows name the same one
- dest_cell: int32 [16, 8, 4096], P('pts', 'nbr'), may hold values from 0 to 8191
- level_input: bfloat16 [128, 512, 16, 128], P('nbr', 'pts'), may hold values from -6 to 6
- w_res: bfloat16 [27, 128, 128], replicated, may hold values from -0.109375 to 0.109375
- w_down: bfloat16 [27, 128, 256], replicated, may hold values from -0.109375 to 0.109375
Outputs:
- lowered: bfloat16 [64, 256, 8, 256], P('nbr', 'pts')
The draws below stay inside these ranges and needn't reach their ends.
Inputs may be any that keep to these rules, and one draw needn't show every extreme that they name: `dest_owner`: at most 64 points of one device go to one owner, and some device sends exactly 64 points to some owner.
All inputs are finite; a program needn't handle non-finite values.
Results may differ from the reference program's by a relative error of at most 0.0048.
Values may be sent and summed in bfloat16 or wider, within the bound.
A program may use at most 64 MiB of HBM per device.

```python
import math
import jax
import jax.numpy as jnp
import numpy as np
from jax import lax

C = 128
C_OUT = 256
BRICK = 16
BX = 1
BY = 2
P_DEV = 4096
CAP = 64
XG = 128
YG = 512
N_PTS = 16
N_NBR = 8
DEVICES = 128


def place_ends(result, rng, low, top_value):
    index_at = [jax.random.randint(jax.random.fold_in(rng, axis), (), 0, length) for axis, length in enumerate(result.shape)]
    longest = result.shape.index(max(result.shape))
    next_to = index_at[:longest] + [(index_at[longest] + 1) % result.shape[longest]] + index_at[longest + 1:]
    return result.at[tuple(index_at)].set(low).at[tuple(next_to)].set(top_value)


def steps_of(key, shape, pieces, smallest, high):
    loudness, own = 1.0, jax.random.fold_in(key, 6)
    for axis_at, parts in pieces:
        heights = jnp.exp(jax.random.uniform(jax.random.fold_in(own, axis_at), (parts,), jnp.float32, smallest / len(pieces), high / len(pieces)))
        loudness = loudness * jnp.repeat(heights, shape[axis_at] // parts).reshape([-1 if axis == axis_at else 1 for axis in range(len(shape))])
    return loudness


def routed_block(key, own, number, rows, number_of, top, reach, slope):
    sequence = jax.random.permutation(key, number_of)
    packed, common = portions_of(number_of, rows * top, reach, slope, True), portions_of(number_of, rows * top, reach, slope, False)
    places = jnp.arange(number_of)

    def named(tallies, rotation):
        used = int((tallies > 0).sum())
        fixed = max(1, used // 4)
        moved = fixed + (places - fixed + rotation * (used - fixed)) % max(1, number_of - fixed)
        return jnp.zeros((number_of,), jnp.int32).at[sequence[jnp.where(places < fixed, places, moved)]].set(jnp.asarray(tallies, jnp.int32))

    tallies = jnp.where(number % 4 == 0, named(packed, number // 4), named(common, number - number // 4 - 1))
    mixed = jax.random.permutation(jax.random.fold_in(own, 3), number_of)
    source_of, taker = mixed[0:number_of // 2 * 2:2], mixed[1:number_of // 2 * 2:2]
    margin = jnp.minimum(tallies[source_of] - 1, reach - tallies[taker]) // 2
    margin = jnp.where((source_of == sequence[0]) | (taker == sequence[0]) | (tallies[taker] == 0), 0, jnp.maximum(margin, 0))
    moved = jax.random.randint(jax.random.fold_in(own, 4), (number_of // 2,), 0, 1 << 20) % (margin + 1)
    tallies = tallies.at[source_of].add(-moved).at[taker].add(moved)
    members = jnp.searchsorted(jnp.cumsum(tallies), jnp.arange(rows * top), side="right").astype(jnp.int32)
    table = members.reshape(top, rows).T
    table = table[jax.random.permutation(jax.random.fold_in(own, 1), rows)]
    rotation = jax.random.randint(jax.random.fold_in(own, 2), (rows, 1), 0, top)
    return jnp.take_along_axis(table, (jnp.arange(top)[None, :] + rotation) % top, axis=1)


def portions_of(number_of, total, reach, lean, full):
    portions = [(1 << 20) // math.isqrt(rank ** lean) + 1 for rank in range(1, number_of + 1)]
    largest = reach if full else min(reach, max(-(-total // number_of), total * portions[0] // sum(portions)))
    least = 1 if total - largest >= number_of - 1 else 0
    holding, spare = [largest] + [least] * (number_of - 1), total - largest - least * (number_of - 1)
    while spare > 0:
        free = [i for i in range(1, number_of) if holding[i] < largest] or [i for i in range(1, number_of) if holding[i] < reach]
        pool, left = sum([portions[i] for i in free]), spare
        for i in free:
            more = min(reach - holding[i], max(1, left * portions[i] // pool), spare)
            holding[i] = holding[i] + more
            spare = spare - more
    return np.array(holding)


def centred(rng, dims, spread, reach, cuts=(), kind=jnp.bfloat16):
    entries = spread * jax.random.normal(rng, dims, jnp.float32)
    if cuts:
        entries = entries * steps_of(rng, dims, cuts, -0.22, 0.18)
    return jnp.clip(entries, -reach, reach).astype(kind)


def setup_inputs(seed: int = 0) -> dict:
    streams_of = jax.random.split(jax.random.key(seed), 7)
    points = centred(streams_of[0], (N_PTS, N_NBR, P_DEV, C), 1.0, 6.0, ((0, 16), (1, 8)))
    dest_owner_keys = jax.random.split(jax.random.fold_in(streams_of[1], 1), N_PTS * N_NBR * P_DEV // P_DEV)
    dest_owner_turns = jax.random.permutation(jax.random.fold_in(streams_of[1], 3), N_PTS * N_NBR * P_DEV // P_DEV)
    dest_owner = jax.vmap(lambda own, number: routed_block(jax.random.fold_in(streams_of[1], 2), own, number, P_DEV, DEVICES, 1, CAP, 2))(dest_owner_keys, dest_owner_turns).reshape((N_PTS, N_NBR, P_DEV, 1))
    dest_cell = place_ends(jax.random.randint(streams_of[2], (N_PTS, N_NBR, P_DEV), 0, BX * BY * BRICK**3), jax.random.fold_in(streams_of[2], 1), 0, (BX * BY * BRICK**3) - 1).astype(jnp.int32)
    level_input = centred(streams_of[3], (XG, YG, BRICK, C), 1.0, 6.0, ((0, 8), (1, 16)))
    w_res = centred(streams_of[4], (27, C, C), (27 * C) ** -0.5, 0.109375)
    w_down = centred(streams_of[5], (27, C, C_OUT), (27 * C) ** -0.5, 0.109375)
    return dict(points=points, dest_owner=dest_owner, dest_cell=dest_cell, level_input=level_input, w_res=w_res, w_down=w_down)


def convolve(source, kernel, stride):
    return lax.conv_general_dilated(source[None], kernel, (stride, stride, stride), ((1, 1), (1, 1), (1, 1)), dimension_numbers=("NDHWC", "DHWIO", "NDHWC"), precision=lax.Precision.HIGHEST)[0]


def reference(points, dest_owner, dest_cell, level_input, w_res, w_down):
    channels = points.shape[-1]
    span_x = BX * BRICK
    span_y = BY * BRICK
    feats = points.reshape(-1, channels).astype(jnp.float32)
    owner = dest_owner.reshape(-1).astype(jnp.int32)
    cell = dest_cell.reshape(-1).astype(jnp.int32)
    cell_x = cell // (span_y * BRICK)
    cell_y = (cell // BRICK) % span_y
    cell_z = cell % BRICK
    glob_x = (owner % N_NBR) * span_x + cell_x
    glob_y = (owner // N_NBR) * span_y + cell_y
    index = ((glob_x * (span_y * N_PTS) + glob_y) * BRICK + cell_z).astype(jnp.int32)
    grid = jnp.zeros((span_x * N_NBR * span_y * N_PTS * BRICK, channels), jnp.float32).at[index].add(feats)
    level = level_input.astype(jnp.float32)
    kernel = w_res.astype(jnp.float32).reshape(3, 3, 3, channels, channels)
    residual = convolve(level, kernel, 1)
    joined = (level + jnp.maximum(residual, 0.0) + grid.reshape(level.shape)).astype(jnp.bfloat16)
    joined = lax.optimization_barrier(joined).astype(jnp.float32)
    down_kernel = w_down.astype(jnp.float32).reshape(3, 3, 3, channels, w_down.shape[-1])
    lowered = convolve(joined, down_kernel, 2)
    return lowered.astype(jnp.bfloat16)
```

```python
import functools

import jax
import jax.numpy as jnp
from jax import lax
from jax.experimental import pallas as pl
from jax.experimental.pallas import tpu as pltpu
from jax.sharding import PartitionSpec as P

MESH = pl.DeviceIdType.MESH
F32, BF16, I32 = jnp.float32, jnp.bfloat16, jnp.int32
DEV, CAP, ROWS, C = 128, 64, 4096, 128
NX, NY, NZ = 16, 32, 16
CELLS = NX * NY * NZ
CHAINS = 4
VMEM = pl.BlockSpec(memory_space=pltpu.VMEM)
SMEM = pl.BlockSpec(memory_space=pltpu.SMEM)
ANY = pl.BlockSpec(memory_space=pl.ANY)


def slots_kernel(own_ref, cell_ref, idx_ref, cells_ref, hit_ref, val_ref):
    block = 256
    hit_ref[...] = (lax.broadcasted_iota(I32, (DEV, ROWS), 0) == own_ref[...]).astype(F32).astype(BF16)
    before = (
        lax.broadcasted_iota(I32, (block, block), 0) < lax.broadcasted_iota(I32, (block, block), 1)
    ).astype(F32).astype(BF16)
    carry = jnp.zeros((DEV, 1), F32)
    for b in range(ROWS // block):
        span = slice(b * block, (b + 1) * block)
        hit = hit_ref[:, span]
        hit32 = hit.astype(F32)
        ranks = jnp.dot(hit, before, preferred_element_type=F32) + carry
        rank = jnp.sum(ranks * hit32, axis=0, keepdims=True).astype(I32)
        carry = carry + jnp.sum(hit32, axis=1, keepdims=True)
        place = lax.broadcasted_iota(I32, (CAP, block), 0) == rank
        row = lax.broadcasted_iota(I32, (1, block), 1) + b * block
        cell = cell_ref[:, span]
        for part, value in enumerate((row % 64, row // 64, cell % 64, cell // 64 + 1)):
            chosen = jnp.where(place, value.astype(F32), 0.0)
            val_ref[part * CAP : (part + 1) * CAP, span] = chosen.astype(BF16)
    found = lax.dot_general(
        hit_ref[...], val_ref[...], (((1,), (1,)), ((), ())), preferred_element_type=F32
    ).astype(I32)
    idx_ref[...] = found[:, CAP : 2 * CAP] * 64 + found[:, :CAP]
    high = found[:, 3 * CAP :]
    cell = (high - 1) * 64 + found[:, 2 * CAP : 3 * CAP]
    cells_ref[:, :CAP] = jnp.where(high > 0, cell, CELLS)
    cells_ref[:, CAP:] = jnp.full((DEV, CAP), CELLS, I32)


def find_slots(own, cell):
    return pl.pallas_call(
        slots_kernel,
        out_shape=(
            jax.ShapeDtypeStruct((DEV, CAP), I32),
            jax.ShapeDtypeStruct((DEV, 2 * CAP), I32),
        ),
        in_specs=[VMEM, VMEM],
        out_specs=(VMEM, VMEM),
        scratch_shapes=[pltpu.VMEM((DEV, ROWS), BF16), pltpu.VMEM((4 * CAP, ROWS), BF16)],
        compiler_params=pltpu.CompilerParams(vmem_limit_bytes=32 << 20),
    )(own, cell)


def partner(k, p, n):
    t = (k * 37) % DEV
    dx, dz, dy, dc = t % 4, (t // 4) % 4, (t // 16) % 4, t // 64
    return (p // 4 + dx) % 4 * 4 + (p % 4 + dz) % 4, (n // 2 + dy) % 4 * 2 + (n % 2 + dc) % 2


def exchange_kernel(
    idx_ref, cells_ref, pts_ref, level_ref, w_ref,
    got_ref, got_cells_ref, base_ref,
    rows32, packed, ext, s0, s1, s2, wide, base,
    row_send, row_recv, cell_send, cell_recv, own_sem, own_cell_sem, in_sem, halo_send, halo_recv, out_sem,
):
    p, n = lax.axis_index("pts"), lax.axis_index("nbr")
    n_p, n_n = lax.axis_size("pts"), lax.axis_size("nbr")
    me = p * n_n + n
    barrier = pltpu.get_barrier_semaphore()

    def greet(k, carry):
        tp, tn = partner(k, p, n)
        pl.semaphore_signal(barrier, inc=1, device_id=(tp, tn), device_id_type=MESH)
        return carry

    lax.fori_loop(1, DEV, greet, 0)
    inner = pltpu.make_async_copy(level_ref, ext.at[pl.ds(1, NX), pl.ds(1, NY)], in_sem)
    inner.start()
    rows32[...] = pts_ref[...].astype(F32)

    def gather(owner):
        for g in range(CAP // 16):
            rows = [rows32[pl.ds(idx_ref[owner, g * 16 + r], 1), :] for r in range(16)]
            packed[owner, g * 16 : (g + 1) * 16, :] = jnp.concatenate(rows, axis=0).astype(BF16)

    gather(me)
    own = pltpu.make_async_copy(packed.at[me], got_ref.at[me], own_sem)
    own.start()
    own_cells = pltpu.make_async_copy(cells_ref.at[me], got_cells_ref.at[me], own_cell_sem)
    own_cells.start()
    pl.semaphore_wait(barrier, DEV - 1)

    sides = []
    for dn in (-1, 0, 1):
        for dp in (-1, 0, 1):
            if dn == 0 and dp == 0:
                continue
            sx = pl.ds(0, NX) if dn == 0 else pl.ds(NX - 1 if dn > 0 else 0, 1)
            sy = pl.ds(0, NY) if dp == 0 else pl.ds(NY - 1 if dp > 0 else 0, 1)
            tx = pl.ds(1, NX) if dn == 0 else pl.ds(0 if dn > 0 else NX + 1, 1)
            ty = pl.ds(1, NY) if dp == 0 else pl.ds(0 if dp > 0 else NY + 1, 1)
            at = len(sides)
            to_n, to_p, from_n, from_p = n + dn, p + dp, n - dn, p - dp
            there = (to_n >= 0) & (to_n < n_n) & (to_p >= 0) & (to_p < n_p)
            here = (from_n >= 0) & (from_n < n_n) & (from_p >= 0) & (from_p < n_p)
            copy = pltpu.make_async_remote_copy(
                level_ref.at[sx, sy], ext.at[tx, ty], halo_send.at[at], halo_recv.at[at],
                device_id=((p + dp + n_p) % n_p, (n + dn + n_n) % n_n), device_id_type=MESH,
            )
            sides.append((there, here, copy, tx, ty))

            @pl.when(there)
            def _():
                copy.start()

    def send(k, carry):
        tp, tn = partner(k, p, n)
        owner = tp * n_n + tn
        gather(owner)
        pltpu.make_async_remote_copy(
            packed.at[owner], got_ref.at[me], row_send, row_recv, device_id=(tp, tn), device_id_type=MESH
        ).start()
        pltpu.make_async_remote_copy(
            cells_ref.at[owner], got_cells_ref.at[me], cell_send, cell_recv,
            device_id=(tp, tn), device_id_type=MESH,
        ).start()
        return carry

    lax.fori_loop(1, DEV, send, 0)

    for a in range(3):
        for q in range(2):
            for c in range(3):
                for pin in range(2):
                    for pout in range(2):
                        b = 2 * q + pin - pout
                        at = (a * 2 + q) * 3 + c
                        tap = w_ref[9 * a + 3 * b + c] if 0 <= b <= 2 else jnp.zeros((C, C), BF16)
                        wide[at * 256 + pin * C : at * 256 + (pin + 1) * C, pout * C : (pout + 1) * C] = tap

    inner.wait()
    for there, here, copy, tx, ty in sides:
        shape = (tx.size, ty.size, NZ, C)

        @pl.when(here)
        def _():
            copy.wait_recv()

        @pl.when(jnp.logical_not(here))
        def _():
            ext[tx, ty] = jnp.zeros(shape, BF16)

    def shift(x, carry):
        for q in range(NY // 2 + 1):
            for part in range(2):
                line = ext[x, 2 * q + part]
                line32 = line.astype(F32)
                edge = jnp.zeros((1, C), F32)
                lanes = slice(part * C, (part + 1) * C)
                s1[x, q, :, lanes] = line
                s0[x, q, :, lanes] = jnp.concatenate([edge, line32[: NZ - 1]], axis=0).astype(BF16)
                s2[x, q, :, lanes] = jnp.concatenate([line32[1:], edge], axis=0).astype(BF16)
        return carry

    lax.fori_loop(0, NX + 2, shift, 0)

    half = NY // 2

    def conv(i, carry):
        lhs = jnp.concatenate(
            [
                s[i + a, q : q + half].reshape(half * NZ, 2 * C)
                for a in range(3)
                for q in range(2)
                for s in (s0, s1, s2)
            ],
            axis=1,
        )
        both = jnp.maximum(jnp.dot(lhs, wide[...], preferred_element_type=F32), 0.0)
        low = s1[i + 1, :half, :, C:].astype(F32)
        high = s1[i + 1, 1:, :, :C].astype(F32)
        base[i, :, 0] = both[:, :C].reshape(half, NZ, C) + low
        base[i, :, 1] = both[:, C:].reshape(half, NZ, C) + high
        pltpu.make_async_copy(base.at[i], base_ref.at[i], out_sem).start()
        return carry

    lax.fori_loop(0, NX, conv, 0)

    pltpu.make_async_copy(base, base_ref, out_sem).wait()
    own.wait()
    own_cells.wait()
    for there, here, copy, tx, ty in sides:

        @pl.when(there)
        def _():
            copy.wait_send()

    most = pl.ds(0, DEV - 1)
    pltpu.make_async_copy(packed.at[most], got_ref.at[most], row_send).wait()
    pltpu.make_async_copy(cells_ref.at[most], got_cells_ref.at[most], cell_send).wait()
    pltpu.make_async_copy(packed.at[most], got_ref.at[most], row_recv).wait()
    pltpu.make_async_copy(cells_ref.at[most], got_cells_ref.at[most], cell_recv).wait()


def exchange(idx, cells, pts, level, w_res):
    dma = pltpu.SemaphoreType.DMA
    padded = (NX + 2, NY // 2 + 1, NZ, 2 * C)
    return pl.pallas_call(
        exchange_kernel,
        out_shape=(
            jax.ShapeDtypeStruct((DEV, CAP, C), BF16),
            jax.ShapeDtypeStruct((DEV, 1, 2 * CAP), I32),
            jax.ShapeDtypeStruct((NX, NY // 2, 2, NZ, C), F32),
        ),
        in_specs=[SMEM, VMEM, VMEM, ANY, VMEM],
        out_specs=(ANY, ANY, ANY),
        scratch_shapes=[
            pltpu.VMEM((ROWS, C), F32),
            pltpu.VMEM((DEV, CAP, C), BF16),
            pltpu.VMEM((NX + 2, NY + 2, NZ, C), BF16),
            pltpu.VMEM(padded, BF16),
            pltpu.VMEM(padded, BF16),
            pltpu.VMEM(padded, BF16),
            pltpu.VMEM((18 * 256, 256), BF16),
            pltpu.VMEM((NX, NY // 2, 2, NZ, C), F32),
            dma, dma, dma, dma, dma, dma, dma, dma((8,)), dma((8,)), dma,
        ],
        compiler_params=pltpu.CompilerParams(
            collective_id=0, has_side_effects=True, vmem_limit_bytes=52 << 20
        ),
    )(idx, cells, pts, level, w_res)


def scatter_kernel(cells_ref, got_ref, base_ref, even_ref, odd_ref, last_ref, rows32, sem, *sums):
    first = pltpu.make_async_copy(base_ref, sums[0].at[pl.ds(0, CELLS)], sem)
    first.start()

    def clear(t, carry):
        span = pl.ds(pl.multiple_of(t * 32, 32), 32)
        for total in sums[1:]:
            total[span, :] = jnp.zeros((32, C), F32)
        rows32[span, :] = got_ref[span, :].astype(F32)
        return carry

    lax.fori_loop(0, CELLS // 32, clear, 0)
    first.wait()
    share = DEV // CHAINS

    def add(s, carry):
        for g in range(CAP // 16):
            for r in range(g * 16, g * 16 + 16):
                at = [cells_ref[k * share + s, r] for k in range(CHAINS)]
                new = [
                    sums[k][pl.ds(at[k], 1), :] + rows32[pl.ds((k * share + s) * CAP + r, 1), :]
                    for k in range(CHAINS)
                ]
                for k in range(CHAINS):
                    sums[k][pl.ds(at[k], 1), :] = new[k]
        return carry

    lax.fori_loop(0, share, add, 0)

    def deal(x, carry):
        top = lax.broadcasted_iota(I32, (NZ // 2, C), 0) == 0

        def total(y, start):
            at = pl.ds((x * NY + y) * NZ + start, NZ // 2, stride=2)
            value = sums[0][at, :]
            for more in sums[1:]:
                value = value + more[at, :]
            return value

        for parity, out_ref in ((0, even_ref), (1, odd_ref)):
            for j in range(0, NY // 2, 2):
                parts = []
                for y in (2 * j + parity, 2 * j + 2 + parity):
                    even, odd = total(y, 0), total(y, 1)
                    below = jnp.where(top, 0.0, pltpu.roll(odd, 1, 0))
                    parts.append((below, even, odd))
                for c in range(3):
                    pair = jnp.concatenate([parts[0][c], parts[1][c]], axis=0).astype(BF16)
                    out_ref[x, j * 8 : j * 8 + 16, c * C : (c + 1) * C] = pair
        return carry

    lax.fori_loop(0, NX, deal, 0)
    for x in range(0, NX, 2):
        parts = [odd_ref[x + h, 112:128, :].astype(F32)[8:] for h in range(2)]
        last_ref[x * 8 : x * 8 + 16, :] = jnp.concatenate(parts, axis=0).astype(BF16)


def scatter(cells, got, base):
    return pl.pallas_call(
        scatter_kernel,
        out_shape=(
            jax.ShapeDtypeStruct((NX, 128, 3 * C), BF16),
            jax.ShapeDtypeStruct((NX, 128, 3 * C), BF16),
            jax.ShapeDtypeStruct((128, 3 * C), BF16),
        ),
        in_specs=[SMEM, VMEM, ANY],
        out_specs=(VMEM, VMEM, VMEM),
        scratch_shapes=[pltpu.VMEM((CELLS, C), F32), pltpu.SemaphoreType.DMA]
        + [pltpu.VMEM((CELLS + 8, C), F32)] * CHAINS,
        compiler_params=pltpu.CompilerParams(vmem_limit_bytes=56 << 20),
    )(cells, got, base)


def lower_kernel(
    even_ref, odd_ref, last_ref, w_ref, out_ref,
    t0, t1, t2, side, corner, send_sem, recv_sem, in_sem,
):
    p, n = lax.axis_index("pts"), lax.axis_index("nbr")
    n_p, n_n = lax.axis_size("pts"), lax.axis_size("nbr")
    barrier = pltpu.get_barrier_semaphore()
    near = ((0, 1), (1, 0), (1, 1))
    up = [((p + dp) % n_p, (n + dn) % n_n) for dp, dn in near]
    down = [((p - dp + n_p) % n_p, (n - dn + n_n) % n_n) for dp, dn in near]
    for device in down:
        pl.semaphore_signal(barrier, inc=1, device_id=device, device_id_type=MESH)
    pl.semaphore_wait(barrier, 3)

    sent = [
        (0, even_ref.at[NX - 1], t1.at[0]),
        (0, odd_ref.at[NX - 1], t2.at[0]),
        (1, last_ref, side),
        (2, last_ref.at[pl.ds(112, 16)], corner),
    ]
    copies = []
    for at, (way, source, target) in enumerate(sent):
        dp, dn = near[way]
        there = (p + dp < n_p) & (n + dn < n_n)
        here = (p - dp >= 0) & (n - dn >= 0)
        copy = pltpu.make_async_remote_copy(
            source, target, send_sem.at[at], recv_sem.at[at], device_id=up[way], device_id_type=MESH
        )
        copies.append((there, here, copy, target))

        @pl.when(there)
        def _():
            copy.start()

    inner = [
        pltpu.make_async_copy(even_ref, t1.at[pl.ds(1, NX)], in_sem.at[0]),
        pltpu.make_async_copy(odd_ref, t2.at[pl.ds(1, NX)], in_sem.at[1]),
    ]
    for copy in inner:
        copy.start()
    for copy in inner:
        copy.wait()
    for there, here, copy, target in copies:

        @pl.when(here)
        def _():
            copy.wait_recv()

        @pl.when(jnp.logical_not(here))
        def _():
            target[...] = jnp.zeros(target.shape, BF16)

    def behind(x, edge):
        line = t2[x].astype(F32)
        t0[x] = jnp.concatenate([edge, line[:120]], axis=0).astype(BF16)

    behind(0, corner[...].astype(F32)[8:])
    for x in range(0, NX, 2):
        edges = side[x * 8 : x * 8 + 16, :].astype(F32)
        behind(x + 1, edges[:8])
        behind(x + 2, edges[8:])

    def conv(i, carry):
        lhs = jnp.concatenate(
            [
                jnp.concatenate([t[4 * i + a], t[4 * i + 2 + a]], axis=0)
                for a in range(3)
                for t in (t0, t1, t2)
            ],
            axis=1,
        )
        low = jnp.dot(lhs, w_ref[...], preferred_element_type=F32).astype(BF16)
        out_ref[2 * i] = low[:128]
        out_ref[2 * i + 1] = low[128:]
        return carry

    lax.fori_loop(0, NX // 4, conv, 0)
    for there, here, copy, target in copies:

        @pl.when(there)
        def _():
            copy.wait_send()


def lower(even, odd, last, w_down):
    dma = pltpu.SemaphoreType.DMA
    return pl.pallas_call(
        lower_kernel,
        out_shape=jax.ShapeDtypeStruct((NX // 2, 128, 2 * C), BF16),
        in_specs=[ANY, ANY, ANY, VMEM],
        out_specs=VMEM,
        scratch_shapes=[pltpu.VMEM((NX + 1, 128, 3 * C), BF16)] * 3
        + [pltpu.VMEM((128, 3 * C), BF16), pltpu.VMEM((16, 3 * C), BF16), dma((4,)), dma((4,)), dma((2,))],
        compiler_params=pltpu.CompilerParams(
            collective_id=1, has_side_effects=True, vmem_limit_bytes=48 << 20
        ),
    )(even, odd, last, w_down)


def body(points, dest_owner, dest_cell, level_input, w_res, w_down):
    idx, cells = find_slots(dest_owner.reshape(1, ROWS), dest_cell.reshape(1, ROWS))
    got, got_cells, base = exchange(
        idx, cells.reshape(DEV, 1, 2 * CAP), points.reshape(ROWS, C), level_input, w_res
    )
    even, odd, last = scatter(
        got_cells.reshape(DEV, 2 * CAP), got.reshape(DEV * CAP, C), base.reshape(CELLS, C)
    )
    lowered = lower(even, odd, last, w_down.reshape(27 * C, 2 * C))
    return lowered.reshape(NX // 2, NY // 2, NZ // 2, 2 * C)


def solution(mesh):
    return jax.shard_map(
        body,
        mesh=mesh,
        in_specs=(
            P("pts", "nbr", None, None),
            P("pts", "nbr", None, None),
            P("pts", "nbr", None),
            P("nbr", "pts", None, None),
            P(),
            P(),
        ),
        out_specs=P("nbr", "pts", None, None),
        check_vma=False,
    )
```

```python
import functools

import jax
import jax.numpy as jnp
from jax import lax
from jax.experimental import pallas as pl
from jax.experimental.pallas import tpu as pltpu
from jax.sharding import PartitionSpec as P

MESH = pl.DeviceIdType.MESH
F32, BF16, I32 = jnp.float32, jnp.bfloat16, jnp.int32
DEV, CAP, ROWS, C = 128, 64, 4096, 128
NX, NY, NZ = 16, 32, 16
CELLS = NX * NY * NZ
CHAINS = 8
VMEM = pl.BlockSpec(memory_space=pltpu.VMEM)
SMEM = pl.BlockSpec(memory_space=pltpu.SMEM)
ANY = pl.BlockSpec(memory_space=pl.ANY)
HBM = pl.BlockSpec(memory_space=pltpu.HBM)


def find_slots(own_ref, cell_ref, hit_ref, val_ref, idx_ref, cells_ref):
    block = 256
    hit_ref[...] = (lax.broadcasted_iota(I32, (DEV, ROWS), 0) == own_ref[...]).astype(F32).astype(BF16)
    before = (
        lax.broadcasted_iota(I32, (block, block), 0) < lax.broadcasted_iota(I32, (block, block), 1)
    ).astype(F32).astype(BF16)
    carry = jnp.zeros((DEV, 1), F32)
    for b in range(ROWS // block):
        span = slice(b * block, (b + 1) * block)
        hit = hit_ref[:, span]
        hit32 = hit.astype(F32)
        ranks = jnp.dot(hit, before, preferred_element_type=F32) + carry
        rank = jnp.sum(ranks * hit32, axis=0, keepdims=True).astype(I32)
        carry = carry + jnp.sum(hit32, axis=1, keepdims=True)
        place = lax.broadcasted_iota(I32, (CAP, block), 0) == rank
        row = lax.broadcasted_iota(I32, (1, block), 1) + b * block + 8
        cell = cell_ref[:, span]
        for part, value in enumerate((row % 64, row // 64, cell % 64, cell // 64)):
            chosen = jnp.where(place, value.astype(F32), 0.0)
            val_ref[part * CAP : (part + 1) * CAP, span] = chosen.astype(BF16)
    found = lax.dot_general(
        hit_ref[...], val_ref[...], (((1,), (1,)), ((), ())), preferred_element_type=F32
    ).astype(I32)
    idx_ref[:, :CAP] = jnp.clip(found[:, CAP : 2 * CAP] * 64 + found[:, :CAP], 0, ROWS + 7)
    idx_ref[:, CAP:] = jnp.zeros((DEV, CAP), I32)
    cells = found[:, 3 * CAP :] * 64 + found[:, 2 * CAP : 3 * CAP]
    cells_ref[...] = jnp.concatenate([cells, jnp.zeros((DEV, CAP), I32)], axis=1).reshape(DEV, 1, 2 * CAP)


def partner(k, p, n):
    t = (k * 37) % DEV
    dx, dz, dy, dc = t % 4, (t // 4) % 4, (t // 16) % 4, t // 64
    return (p // 4 + dx) % 4 * 4 + (p % 4 + dz) % 4, (n // 2 + dy) % 4 * 2 + (n % 2 + dc) % 2


def exchange_kernel(
    own_hbm, cell_hbm, pts_hbm, level_ref, w_hbm,
    got_ref, got_cells_ref, base,
    owner_of, cell_of, hit, val, idx_vmem, idx_ref, cells_ref, pts, taps, rows32, packed, ext, s0, s1, s2, wide,
    row_send, row_recv, cell_send, cell_recv, own_sem, own_cell_sem, in_sem, pts_sem, taps_sem, list_sem, halo_send, halo_recv,
):
    p, n = lax.axis_index("pts"), lax.axis_index("nbr")
    n_p, n_n = lax.axis_size("pts"), lax.axis_size("nbr")
    me = p * n_n + n
    barrier = pltpu.get_barrier_semaphore()
    lists_in = [
        pltpu.make_async_copy(own_hbm, owner_of, list_sem.at[0]),
        pltpu.make_async_copy(cell_hbm, cell_of, list_sem.at[1]),
    ]
    pts_in = pltpu.make_async_copy(pts_hbm, pts, pts_sem)
    for copy in lists_in:
        copy.start()
    pts_in.start()

    def greet(k, carry):
        for d in range(n_n):
            device = ((p + k) % n_p, (n + d) % n_n)
            pl.semaphore_signal(barrier, inc=1, device_id=device, device_id_type=MESH)
        return carry

    for d in range(1, n_n):
        pl.semaphore_signal(barrier, inc=1, device_id=(p, (n + d) % n_n), device_id_type=MESH)
    lax.fori_loop(1, n_p, greet, 0)
    inner = pltpu.make_async_copy(level_ref, ext.at[pl.ds(1, NX), pl.ds(1, NY)], in_sem)
    inner.start()
    taps_in = pltpu.make_async_copy(w_hbm, taps, taps_sem)
    taps_in.start()
    for copy in lists_in:
        copy.wait()
    find_slots(owner_of, cell_of, hit, val, idx_vmem, cells_ref)
    idx_in = pltpu.make_async_copy(idx_vmem, idx_ref, list_sem.at[2])
    idx_in.start()
    rows32[:8, :] = jnp.zeros((8, C), F32)
    pts_in.wait()
    rows32[8:, :] = pts[...].astype(F32)
    idx_in.wait()

    def gather(owner):
        for g in range(CAP // 16):
            rows = [rows32[pl.ds(idx_ref[owner, g * 16 + r], 1), :] for r in range(16)]
            packed[owner, g * 16 : (g + 1) * 16, :] = jnp.concatenate(rows, axis=0).astype(BF16)

    gather(me)
    own = pltpu.make_async_copy(packed.at[me], got_ref.at[me], own_sem)
    own.start()
    own_cells = pltpu.make_async_copy(cells_ref.at[me], got_cells_ref.at[me], own_cell_sem)
    own_cells.start()
    pl.semaphore_wait(barrier, DEV - 1)

    sides = []
    for dn in (-1, 0, 1):
        for dp in (-1, 0, 1):
            if dn == 0 and dp == 0:
                continue
            sx = pl.ds(0, NX) if dn == 0 else pl.ds(NX - 1 if dn > 0 else 0, 1)
            sy = pl.ds(0, NY) if dp == 0 else pl.ds(NY - 1 if dp > 0 else 0, 1)
            tx = pl.ds(1, NX) if dn == 0 else pl.ds(0 if dn > 0 else NX + 1, 1)
            ty = pl.ds(1, NY) if dp == 0 else pl.ds(0 if dp > 0 else NY + 1, 1)
            at = len(sides)
            to_n, to_p, from_n, from_p = n + dn, p + dp, n - dn, p - dp
            there = (to_n >= 0) & (to_n < n_n) & (to_p >= 0) & (to_p < n_p)
            here = (from_n >= 0) & (from_n < n_n) & (from_p >= 0) & (from_p < n_p)
            copy = pltpu.make_async_remote_copy(
                level_ref.at[sx, sy], ext.at[tx, ty], halo_send.at[at], halo_recv.at[at],
                device_id=((p + dp + n_p) % n_p, (n + dn + n_n) % n_n), device_id_type=MESH,
            )
            sides.append((there, here, copy, tx, ty))

            @pl.when(there)
            def _():
                copy.start()

    def send(k, carry):
        tp, tn = partner(k, p, n)
        owner = tp * n_n + tn
        gather(owner)
        pltpu.make_async_remote_copy(
            packed.at[owner], got_ref.at[me], row_send, row_recv, device_id=(tp, tn), device_id_type=MESH
        ).start()
        pltpu.make_async_remote_copy(
            cells_ref.at[owner], got_cells_ref.at[me], cell_send, cell_recv,
            device_id=(tp, tn), device_id_type=MESH,
        ).start()
        return carry

    lax.fori_loop(1, DEV, send, 0)

    taps_in.wait()
    for a in range(3):
        for q in range(2):
            for c in range(3):
                for pin in range(2):
                    for pout in range(2):
                        b = 2 * q + pin - pout
                        at = (a * 2 + q) * 3 + c
                        tap = taps[9 * a + 3 * b + c] if 0 <= b <= 2 else jnp.zeros((C, C), BF16)
                        wide[at * 256 + pin * C : at * 256 + (pin + 1) * C, pout * C : (pout + 1) * C] = tap

    inner.wait()
    for there, here, copy, tx, ty in sides:
        shape = (tx.size, ty.size, NZ, C)

        @pl.when(here)
        def _():
            copy.wait_recv()

        @pl.when(jnp.logical_not(here))
        def _():
            ext[tx, ty] = jnp.zeros(shape, BF16)

    def shift(x, carry):
        for q in range(NY // 2 + 1):
            for part in range(2):
                line = ext[x, 2 * q + part]
                line32 = line.astype(F32)
                edge = jnp.zeros((1, C), F32)
                lanes = slice(part * C, (part + 1) * C)
                s1[x, q, :, lanes] = line
                s0[x, q, :, lanes] = jnp.concatenate([edge, line32[: NZ - 1]], axis=0).astype(BF16)
                s2[x, q, :, lanes] = jnp.concatenate([line32[1:], edge], axis=0).astype(BF16)
        return carry

    lax.fori_loop(0, NX + 2, shift, 0)

    half = NY // 2

    def conv(i, carry):
        lhs = jnp.concatenate(
            [
                s[i + a, q : q + half].reshape(half * NZ, 2 * C)
                for a in range(3)
                for q in range(2)
                for s in (s0, s1, s2)
            ],
            axis=1,
        )
        both = jnp.maximum(jnp.dot(lhs, wide[...], preferred_element_type=F32), 0.0)
        low = s1[i + 1, :half, :, C:].astype(F32)
        high = s1[i + 1, 1:, :, :C].astype(F32)
        base[i, :, 0] = both[:, :C].reshape(half, NZ, C) + low
        base[i, :, 1] = both[:, C:].reshape(half, NZ, C) + high
        return carry

    lax.fori_loop(0, NX, conv, 0)

    own.wait()
    own_cells.wait()
    for there, here, copy, tx, ty in sides:

        @pl.when(there)
        def _():
            copy.wait_send()

    most = pl.ds(0, DEV - 1)
    pltpu.make_async_copy(packed.at[most], got_ref.at[most], row_send).wait()
    pltpu.make_async_copy(cells_ref.at[most], got_cells_ref.at[most], cell_send).wait()
    pltpu.make_async_copy(packed.at[most], got_ref.at[most], row_recv).wait()
    pltpu.make_async_copy(cells_ref.at[most], got_cells_ref.at[most], cell_recv).wait()


def exchange(own, cell, pts, level, w_res):
    dma = pltpu.SemaphoreType.DMA
    padded = (NX + 2, NY // 2 + 1, NZ, 2 * C)
    return pl.pallas_call(
        exchange_kernel,
        out_shape=(
            jax.ShapeDtypeStruct((DEV, CAP, C), BF16),
            jax.ShapeDtypeStruct((DEV, 1, 2 * CAP), I32),
            jax.ShapeDtypeStruct((NX, NY // 2, 2, NZ, C), F32),
        ),
        in_specs=[HBM, HBM, HBM, HBM, HBM],
        out_specs=(VMEM, VMEM, VMEM),
        scratch_shapes=[
            pltpu.VMEM((1, ROWS), I32),
            pltpu.VMEM((1, ROWS), I32),
            pltpu.VMEM((DEV, ROWS), BF16),
            pltpu.VMEM((4 * CAP, ROWS), BF16),
            pltpu.VMEM((DEV, 2 * CAP), I32),
            pltpu.SMEM((DEV, 2 * CAP), I32),
            pltpu.VMEM((DEV, 1, 2 * CAP), I32),
            pltpu.VMEM((ROWS, C), BF16),
            pltpu.VMEM((27, C, C), BF16),
            pltpu.VMEM((ROWS + 8, C), F32),
            pltpu.VMEM((DEV, CAP, C), BF16),
            pltpu.VMEM((NX + 2, NY + 2, NZ, C), BF16),
            pltpu.VMEM(padded, BF16),
            pltpu.VMEM(padded, BF16),
            pltpu.VMEM(padded, BF16),
            pltpu.VMEM((18 * 256, 256), BF16),
            dma, dma, dma, dma, dma, dma, dma, dma, dma, dma((3,)), dma((8,)), dma((8,)),
        ],
        compiler_params=pltpu.CompilerParams(
            collective_id=0, has_side_effects=True, vmem_limit_bytes=36 << 20
        ),
    )(*(pltpu.with_memory_space_constraint(x, pltpu.HBM) for x in (own, cell, pts, level, w_res)))


def scatter_kernel(cells_ref, got_ref, base_ref, even_ref, odd_ref, last_ref, rows32, *sums):

    def clear(t, carry):
        span = pl.ds(pl.multiple_of(t * 32, 32), 32)
        for total in sums:
            total[span, :] = jnp.zeros((32, C), F32)
        rows32[span, :] = got_ref[span, :].astype(F32)
        return carry

    lax.fori_loop(0, CELLS // 32, clear, 0)
    share = DEV // CHAINS

    def add(s, carry):
        for g in range(CAP // 16):
            for r in range(g * 16, g * 16 + 16):
                at = [cells_ref[(k * share + s) * (2 * CAP) + r] for k in range(CHAINS)]
                new = [
                    sums[k][pl.ds(at[k], 1), :] + rows32[pl.ds((k * share + s) * CAP + r, 1), :]
                    for k in range(CHAINS)
                ]
                for k in range(CHAINS):
                    sums[k][pl.ds(at[k], 1), :] = new[k]
        return carry

    lax.fori_loop(0, share, add, 0)

    def deal(x, carry):
        top = lax.broadcasted_iota(I32, (NZ // 2, C), 0) == 0

        def total(y, start):
            at = pl.ds((x * NY + y) * NZ + start, NZ // 2, stride=2)
            value = base_ref[at, :]
            for more in sums:
                value = value + more[at, :]
            return value

        for parity, out_ref in ((0, even_ref), (1, odd_ref)):
            for j in range(0, NY // 2, 2):
                parts = []
                for y in (2 * j + parity, 2 * j + 2 + parity):
                    even, odd = total(y, 0), total(y, 1)
                    below = jnp.where(top, 0.0, pltpu.roll(odd, 1, 0))
                    parts.append((below, even, odd))
                for c in range(3):
                    pair = jnp.concatenate([parts[0][c], parts[1][c]], axis=0).astype(BF16)
                    out_ref[x, j * 8 : j * 8 + 16, c * C : (c + 1) * C] = pair
        return carry

    lax.fori_loop(0, NX, deal, 0)
    for x in range(0, NX, 2):
        parts = [odd_ref[x + h, 112:128, :].astype(F32)[8:] for h in range(2)]
        last_ref[x * 8 : x * 8 + 16, :] = jnp.concatenate(parts, axis=0).astype(BF16)


def scatter(cells, got, base):
    return pl.pallas_call(
        scatter_kernel,
        out_shape=(
            jax.ShapeDtypeStruct((NX, 128, 3 * C), BF16),
            jax.ShapeDtypeStruct((NX, 128, 3 * C), BF16),
            jax.ShapeDtypeStruct((128, 3 * C), BF16),
        ),
        in_specs=[SMEM, VMEM, VMEM],
        out_specs=(VMEM, VMEM, VMEM),
        scratch_shapes=[pltpu.VMEM((CELLS, C), F32)] * (1 + CHAINS),
        compiler_params=pltpu.CompilerParams(vmem_limit_bytes=40 << 20),
    )(cells, got, base)


def lower_kernel(
    even_ref, odd_ref, last_ref, w_ref, out_ref,
    behind_odd, front_even, front_odd, side, corner, total, send_sem, recv_sem,
):
    p, n = lax.axis_index("pts"), lax.axis_index("nbr")
    n_p, n_n = lax.axis_size("pts"), lax.axis_size("nbr")
    barrier = pltpu.get_barrier_semaphore()
    near = ((0, 1), (1, 0), (1, 1))
    up = [((p + dp) % n_p, (n + dn) % n_n) for dp, dn in near]
    down = [((p - dp + n_p) % n_p, (n - dn + n_n) % n_n) for dp, dn in near]
    for device in down:
        pl.semaphore_signal(barrier, inc=1, device_id=device, device_id_type=MESH)
    pl.semaphore_wait(barrier, 3)

    sent = [
        (0, even_ref.at[NX - 1], front_even),
        (0, odd_ref.at[NX - 1], front_odd),
        (1, last_ref, side),
        (2, last_ref.at[pl.ds(112, 16)], corner),
    ]
    copies = []
    for at, (way, source, target) in enumerate(sent):
        dp, dn = near[way]
        there = (p + dp < n_p) & (n + dn < n_n)
        here = (p - dp >= 0) & (n - dn >= 0)
        copy = pltpu.make_async_remote_copy(
            source, target, send_sem.at[at], recv_sem.at[at], device_id=up[way], device_id_type=MESH
        )
        copies.append((there, here, copy, target))

        @pl.when(there)
        def _():
            copy.start()

    taps = 3 * C

    def inner(x):
        return jnp.concatenate([even_ref[x], odd_ref[x]], axis=1)

    def weights(a):
        return w_ref[(3 * a + 1) * taps : (3 * a + 3) * taps, :]

    for i in range(0, NX // 2, 2):
        acc = jnp.zeros((256, 2 * C), F32)
        for a in (1, 2):
            lhs = jnp.concatenate([inner(2 * i + a - 1), inner(2 * i + a + 1)], axis=0)
            acc = acc + jnp.dot(lhs, weights(a), preferred_element_type=F32)
        if i:
            lhs = jnp.concatenate([inner(2 * i - 1), inner(2 * i + 1)], axis=0)
            acc = acc + jnp.dot(lhs, weights(0), preferred_element_type=F32)
            total[i] = acc[:128]
            total[i + 1] = acc[128:]
        else:
            total[0] = acc[:128]
            total[1] = acc[128:] + jnp.dot(inner(1), weights(0), preferred_element_type=F32)

    for x in range(NX):
        line = odd_ref[x].astype(F32)
        behind_odd[x + 1, 16:, :] = line[8:120].astype(BF16)

    for there, here, copy, target in copies:

        @pl.when(here)
        def _():
            copy.wait_recv()

        @pl.when(jnp.logical_not(here))
        def _():
            target[...] = jnp.zeros(target.shape, BF16)

    front = front_odd[...].astype(F32)
    behind_odd[0] = jnp.concatenate([corner[...].astype(F32)[8:], front[:120]], axis=0).astype(BF16)
    for x in range(0, NX, 2):
        edges = side[x * 8 : x * 8 + 16, :].astype(F32)
        for h in range(2):
            line = odd_ref[x + h, 0:16, :].astype(F32)[:8]
            behind_odd[x + h + 1, 0:16, :] = jnp.concatenate([edges[8 * h : 8 * h + 8], line], axis=0).astype(BF16)

    ahead = jnp.concatenate([front_even[...], front_odd[...]], axis=1)
    total[0] += jnp.dot(ahead, weights(0), preferred_element_type=F32)
    for i in range(0, NX // 2, 2):
        lhs = jnp.concatenate(
            [
                jnp.concatenate([behind_odd[2 * i + a], behind_odd[2 * i + 2 + a]], axis=0)
                for a in range(3)
            ],
            axis=1,
        )
        rest = jnp.concatenate([w_ref[3 * a * taps : (3 * a + 1) * taps, :] for a in range(3)], axis=0)
        low = jnp.dot(lhs, rest, preferred_element_type=F32)
        out_ref[i] = (total[i] + low[:128]).astype(BF16)
        out_ref[i + 1] = (total[i + 1] + low[128:]).astype(BF16)
    for there, here, copy, target in copies:

        @pl.when(there)
        def _():
            copy.wait_send()


def lower(even, odd, last, w_down):
    dma = pltpu.SemaphoreType.DMA
    return pl.pallas_call(
        lower_kernel,
        out_shape=jax.ShapeDtypeStruct((NX // 2, 128, 2 * C), BF16),
        in_specs=[VMEM, VMEM, VMEM, VMEM],
        out_specs=VMEM,
        scratch_shapes=[
            pltpu.VMEM((NX + 1, 128, 3 * C), BF16),
            pltpu.VMEM((128, 3 * C), BF16),
            pltpu.VMEM((128, 3 * C), BF16),
            pltpu.VMEM((128, 3 * C), BF16),
            pltpu.VMEM((16, 3 * C), BF16),
            pltpu.VMEM((NX // 2, 128, 2 * C), F32),
            dma((4,)),
            dma((4,)),
        ],
        compiler_params=pltpu.CompilerParams(
            collective_id=1, has_side_effects=True, vmem_limit_bytes=24 << 20
        ),
    )(even, odd, last, w_down)


def body(points, dest_owner, dest_cell, level_input, w_res, w_down):
    got, got_cells, base = exchange(
        dest_owner.reshape(1, ROWS), dest_cell.reshape(1, ROWS), points.reshape(ROWS, C), level_input, w_res
    )
    even, odd, last = scatter(
        got_cells.reshape(DEV * 2 * CAP), got.reshape(DEV * CAP, C), base.reshape(CELLS, C)
    )
    lowered = lower(even, odd, last, w_down.reshape(27 * C, 2 * C))
    return lowered.reshape(NX // 2, NY // 2, NZ // 2, 2 * C)


def solution(mesh):
    return jax.shard_map(
        body,
        mesh=mesh,
        in_specs=(
            P("pts", "nbr", None, None),
            P("pts", "nbr", None, None),
            P("pts", "nbr", None),
            P("nbr", "pts", None, None),
            P(),
            P(),
        ),
        out_specs=P("nbr", "pts", None, None),
        check_vma=False,
    )
```

```python
import functools

import jax
import jax.numpy as jnp
from jax import lax
from jax.experimental import pallas as pl
from jax.experimental.pallas import tpu as pltpu
from jax.sharding import PartitionSpec as P

MESH = pl.DeviceIdType.MESH
F32, BF16, I32 = jnp.float32, jnp.bfloat16, jnp.int32
DEV, CAP, ROWS, C = 128, 64, 4096, 128
NX, NY, NZ = 16, 32, 16
CELLS = NX * NY * NZ
CHAINS = 8
VMEM = pl.BlockSpec(memory_space=pltpu.VMEM)
SMEM = pl.BlockSpec(memory_space=pltpu.SMEM)
ANY = pl.BlockSpec(memory_space=pl.ANY)
HBM = pl.BlockSpec(memory_space=pltpu.HBM)


def find_slots(own_ref, cell_ref, hit_ref, val_ref, idx_ref, cells_ref):
    block = 256
    hit_ref[...] = (lax.broadcasted_iota(I32, (DEV, ROWS), 0) == own_ref[...]).astype(F32).astype(BF16)
    before = (
        lax.broadcasted_iota(I32, (block, block), 0) < lax.broadcasted_iota(I32, (block, block), 1)
    ).astype(F32).astype(BF16)
    carry = jnp.zeros((DEV, 1), F32)
    for b in range(ROWS // block):
        span = slice(b * block, (b + 1) * block)
        hit = hit_ref[:, span]
        hit32 = hit.astype(F32)
        ranks = jnp.dot(hit, before, preferred_element_type=F32) + carry
        rank = jnp.sum(ranks * hit32, axis=0, keepdims=True).astype(I32)
        carry = carry + jnp.sum(hit32, axis=1, keepdims=True)
        place = lax.broadcasted_iota(I32, (CAP, block), 0) == rank
        row = lax.broadcasted_iota(I32, (1, block), 1) + b * block + 8
        cell = cell_ref[:, span]
        for part, value in enumerate((row % 64, row // 64, cell % 64, cell // 64)):
            chosen = jnp.where(place, value.astype(F32), 0.0)
            val_ref[part * CAP : (part + 1) * CAP, span] = chosen.astype(BF16)
    found = lax.dot_general(
        hit_ref[...], val_ref[...], (((1,), (1,)), ((), ())), preferred_element_type=F32
    ).astype(I32)
    idx_ref[:, :CAP] = jnp.clip(found[:, CAP : 2 * CAP] * 64 + found[:, :CAP], 0, ROWS + 7)
    idx_ref[:, CAP:] = jnp.zeros((DEV, CAP), I32)
    cells = found[:, 3 * CAP :] * 64 + found[:, 2 * CAP : 3 * CAP]
    full = found[:, CAP : 2 * CAP] + found[:, :CAP] > 0
    cells = jnp.where(full, cells, lax.broadcasted_iota(I32, (DEV, CAP), 1) * NZ)
    cells_ref[...] = jnp.concatenate([cells, jnp.zeros((DEV, CAP), I32)], axis=1).reshape(DEV, 1, 2 * CAP)


def partner(k, p, n):
    t = (k * 37) % DEV
    dx, dz, dy, dc = t % 4, (t // 4) % 4, (t // 16) % 4, t // 64
    return (p // 4 + dx) % 4 * 4 + (p % 4 + dz) % 4, (n // 2 + dy) % 4 * 2 + (n % 2 + dc) % 2


def exchange_kernel(
    own_hbm, cell_hbm, pts_hbm, level_ref, w_hbm,
    got_ref, got_cells_ref, base,
    owner_of, cell_of, hit, val, idx_vmem, idx_ref, cells_ref, pts, taps, rows32, packed, ext, s0, s1, s2, wide,
    row_send, row_recv, cell_send, cell_recv, own_sem, own_cell_sem, in_sem, pts_sem, taps_sem, list_sem, halo_send, halo_recv,
):
    p, n = lax.axis_index("pts"), lax.axis_index("nbr")
    n_p, n_n = lax.axis_size("pts"), lax.axis_size("nbr")
    me = p * n_n + n
    barrier = pltpu.get_barrier_semaphore()
    lists_in = [
        pltpu.make_async_copy(own_hbm, owner_of, list_sem.at[0]),
        pltpu.make_async_copy(cell_hbm, cell_of, list_sem.at[1]),
    ]
    pts_in = pltpu.make_async_copy(pts_hbm, pts, pts_sem)
    for copy in lists_in:
        copy.start()
    pts_in.start()

    def greet(k, carry):
        for d in range(n_n):
            device = ((p + k) % n_p, (n + d) % n_n)
            pl.semaphore_signal(barrier, inc=1, device_id=device, device_id_type=MESH)
        return carry

    for d in range(1, n_n):
        pl.semaphore_signal(barrier, inc=1, device_id=(p, (n + d) % n_n), device_id_type=MESH)
    lax.fori_loop(1, n_p, greet, 0)
    inner = pltpu.make_async_copy(level_ref, ext.at[pl.ds(1, NX), pl.ds(1, NY)], in_sem)
    inner.start()
    taps_in = pltpu.make_async_copy(w_hbm, taps, taps_sem)
    taps_in.start()
    for copy in lists_in:
        copy.wait()
    find_slots(owner_of, cell_of, hit, val, idx_vmem, cells_ref)
    idx_in = pltpu.make_async_copy(idx_vmem, idx_ref, list_sem.at[2])
    idx_in.start()
    rows32[:8, :] = jnp.zeros((8, C), F32)
    pts_in.wait()
    rows32[8:, :] = pts[...].astype(F32)
    idx_in.wait()

    def gather(owner):
        for g in range(CAP // 16):
            rows = [rows32[pl.ds(idx_ref[owner, g * 16 + r], 1), :] for r in range(16)]
            packed[owner, g * 16 : (g + 1) * 16, :] = jnp.concatenate(rows, axis=0).astype(BF16)

    gather(me)
    own = pltpu.make_async_copy(packed.at[me], got_ref.at[me], own_sem)
    own.start()
    own_cells = pltpu.make_async_copy(cells_ref.at[me], got_cells_ref.at[me], own_cell_sem)
    own_cells.start()
    pl.semaphore_wait(barrier, DEV - 1)

    sides = []
    for dn in (-1, 0, 1):
        for dp in (-1, 0, 1):
            if dn == 0 and dp == 0:
                continue
            sx = pl.ds(0, NX) if dn == 0 else pl.ds(NX - 1 if dn > 0 else 0, 1)
            sy = pl.ds(0, NY) if dp == 0 else pl.ds(NY - 1 if dp > 0 else 0, 1)
            tx = pl.ds(1, NX) if dn == 0 else pl.ds(0 if dn > 0 else NX + 1, 1)
            ty = pl.ds(1, NY) if dp == 0 else pl.ds(0 if dp > 0 else NY + 1, 1)
            at = len(sides)
            to_n, to_p, from_n, from_p = n + dn, p + dp, n - dn, p - dp
            there = (to_n >= 0) & (to_n < n_n) & (to_p >= 0) & (to_p < n_p)
            here = (from_n >= 0) & (from_n < n_n) & (from_p >= 0) & (from_p < n_p)
            copy = pltpu.make_async_remote_copy(
                level_ref.at[sx, sy], ext.at[tx, ty], halo_send.at[at], halo_recv.at[at],
                device_id=((p + dp + n_p) % n_p, (n + dn + n_n) % n_n), device_id_type=MESH,
            )
            sides.append((there, here, copy, tx, ty))

            @pl.when(there)
            def _():
                copy.start()

    def send(k, carry):
        tp, tn = partner(k, p, n)
        owner = tp * n_n + tn
        gather(owner)
        pltpu.make_async_remote_copy(
            packed.at[owner], got_ref.at[me], row_send, row_recv, device_id=(tp, tn), device_id_type=MESH
        ).start()
        pltpu.make_async_remote_copy(
            cells_ref.at[owner], got_cells_ref.at[me], cell_send, cell_recv,
            device_id=(tp, tn), device_id_type=MESH,
        ).start()
        return carry

    lax.fori_loop(1, DEV, send, 0)

    taps_in.wait()
    for a in range(3):
        for q in range(2):
            for c in range(3):
                for pin in range(2):
                    for pout in range(2):
                        b = 2 * q + pin - pout
                        at = (a * 2 + q) * 3 + c
                        tap = taps[9 * a + 3 * b + c] if 0 <= b <= 2 else jnp.zeros((C, C), BF16)
                        wide[at * 256 + pin * C : at * 256 + (pin + 1) * C, pout * C : (pout + 1) * C] = tap

    inner.wait()
    for there, here, copy, tx, ty in sides:
        shape = (tx.size, ty.size, NZ, C)

        @pl.when(here)
        def _():
            copy.wait_recv()

        @pl.when(jnp.logical_not(here))
        def _():
            ext[tx, ty] = jnp.zeros(shape, BF16)

    def shift(x, carry):
        for q in range(NY // 2 + 1):
            for part in range(2):
                line = ext[x, 2 * q + part]
                line32 = line.astype(F32)
                edge = jnp.zeros((1, C), F32)
                lanes = slice(part * C, (part + 1) * C)
                s1[x, q, :, lanes] = line
                s0[x, q, :, lanes] = jnp.concatenate([edge, line32[: NZ - 1]], axis=0).astype(BF16)
                s2[x, q, :, lanes] = jnp.concatenate([line32[1:], edge], axis=0).astype(BF16)
        return carry

    lax.fori_loop(0, NX + 2, shift, 0)

    half = NY // 2

    def conv(i, carry):
        lhs = jnp.concatenate(
            [
                s[i + a, q : q + half].reshape(half * NZ, 2 * C)
                for a in range(3)
                for q in range(2)
                for s in (s0, s1, s2)
            ],
            axis=1,
        )
        both = jnp.maximum(jnp.dot(lhs, wide[...], preferred_element_type=F32), 0.0)
        low = s1[i + 1, :half, :, C:].astype(F32)
        high = s1[i + 1, 1:, :, :C].astype(F32)
        base[i, :, 0] = both[:, :C].reshape(half, NZ, C) + low
        base[i, :, 1] = both[:, C:].reshape(half, NZ, C) + high
        return carry

    lax.fori_loop(0, NX, conv, 0)

    own.wait()
    own_cells.wait()
    for there, here, copy, tx, ty in sides:

        @pl.when(there)
        def _():
            copy.wait_send()

    most = pl.ds(0, DEV - 1)
    pltpu.make_async_copy(packed.at[most], got_ref.at[most], row_send).wait()
    pltpu.make_async_copy(cells_ref.at[most], got_cells_ref.at[most], cell_send).wait()
    pltpu.make_async_copy(packed.at[most], got_ref.at[most], row_recv).wait()
    pltpu.make_async_copy(cells_ref.at[most], got_cells_ref.at[most], cell_recv).wait()


def exchange(own, cell, pts, level, w_res):
    dma = pltpu.SemaphoreType.DMA
    padded = (NX + 2, NY // 2 + 1, NZ, 2 * C)
    return pl.pallas_call(
        exchange_kernel,
        out_shape=(
            jax.ShapeDtypeStruct((DEV, CAP, C), BF16),
            jax.ShapeDtypeStruct((DEV, 1, 2 * CAP), I32),
            jax.ShapeDtypeStruct((NX, NY // 2, 2, NZ, C), F32),
        ),
        in_specs=[HBM, HBM, HBM, HBM, HBM],
        out_specs=(VMEM, VMEM, VMEM),
        scratch_shapes=[
            pltpu.VMEM((1, ROWS), I32),
            pltpu.VMEM((1, ROWS), I32),
            pltpu.VMEM((DEV, ROWS), BF16),
            pltpu.VMEM((4 * CAP, ROWS), BF16),
            pltpu.VMEM((DEV, 2 * CAP), I32),
            pltpu.SMEM((DEV, 2 * CAP), I32),
            pltpu.VMEM((DEV, 1, 2 * CAP), I32),
            pltpu.VMEM((ROWS, C), BF16),
            pltpu.VMEM((27, C, C), BF16),
            pltpu.VMEM((ROWS + 8, C), F32),
            pltpu.VMEM((DEV, CAP, C), BF16),
            pltpu.VMEM((NX + 2, NY + 2, NZ, C), BF16),
            pltpu.VMEM(padded, BF16),
            pltpu.VMEM(padded, BF16),
            pltpu.VMEM(padded, BF16),
            pltpu.VMEM((18 * 256, 256), BF16),
            dma, dma, dma, dma, dma, dma, dma, dma, dma, dma((3,)), dma((8,)), dma((8,)),
        ],
        compiler_params=pltpu.CompilerParams(
            collective_id=0, has_side_effects=True, vmem_limit_bytes=36 << 20
        ),
    )(*(pltpu.with_memory_space_constraint(x, pltpu.HBM) for x in (own, cell, pts, level, w_res)))


def scatter_kernel(cells_in, got_ref, base_ref, even_ref, odd_ref, last_ref, cells_ref, sem, rows32, *sums):
    listed = pltpu.make_async_copy(cells_in, cells_ref, sem)
    listed.start()

    def clear(t, carry):
        span = pl.ds(pl.multiple_of(t * 32, 32), 32)
        for total in sums:
            total[span, :] = jnp.zeros((32, C), F32)
        rows32[span, :] = got_ref[span, :].astype(F32)
        return carry

    lax.fori_loop(0, CELLS // 32, clear, 0)
    share = DEV // CHAINS
    listed.wait()

    def add(s, carry):
        for g in range(CAP // 16):
            for r in range(g * 16, g * 16 + 16):
                at = [cells_ref[(k * share + s) * (2 * CAP) + r] for k in range(CHAINS)]
                new = [
                    sums[k][pl.ds(at[k], 1), :] + rows32[pl.ds((k * share + s) * CAP + r, 1), :]
                    for k in range(CHAINS)
                ]
                for k in range(CHAINS):
                    sums[k][pl.ds(at[k], 1), :] = new[k]
        return carry

    lax.fori_loop(0, share, add, 0)

    def deal(x, carry):
        top = lax.broadcasted_iota(I32, (NZ // 2, C), 0) == 0

        def total(y, start):
            at = pl.ds((x * NY + y) * NZ + start, NZ // 2, stride=2)
            value = base_ref[at, :]
            for more in sums:
                value = value + more[at, :]
            return value

        for parity, out_ref in ((0, even_ref), (1, odd_ref)):
            for j in range(0, NY // 2, 2):
                parts = []
                for y in (2 * j + parity, 2 * j + 2 + parity):
                    even, odd = total(y, 0), total(y, 1)
                    below = jnp.where(top, 0.0, pltpu.roll(odd, 1, 0))
                    parts.append((below, even, odd))
                for c in range(3):
                    pair = jnp.concatenate([parts[0][c], parts[1][c]], axis=0).astype(BF16)
                    out_ref[x, j * 8 : j * 8 + 16, c * C : (c + 1) * C] = pair
        return carry

    lax.fori_loop(0, NX, deal, 0)
    for x in range(0, NX, 2):
        parts = [odd_ref[x + h, 112:128, C:].astype(F32)[8:] for h in range(2)]
        last_ref[x * 8 : x * 8 + 16, :] = jnp.concatenate(parts, axis=0).astype(BF16)


def scatter(cells, got, base):
    return pl.pallas_call(
        scatter_kernel,
        out_shape=(
            jax.ShapeDtypeStruct((NX, 128, 3 * C), BF16),
            jax.ShapeDtypeStruct((NX, 128, 3 * C), BF16),
            jax.ShapeDtypeStruct((128, 2 * C), BF16),
        ),
        in_specs=[ANY, VMEM, VMEM],
        out_specs=(VMEM, VMEM, VMEM),
        scratch_shapes=[pltpu.SMEM((DEV * 2 * CAP,), I32), pltpu.SemaphoreType.DMA]
        + [pltpu.VMEM((CELLS, C), F32)] * (1 + CHAINS),
        compiler_params=pltpu.CompilerParams(vmem_limit_bytes=40 << 20),
    )(cells, got, base)


def lower_kernel(
    even_ref, odd_ref, last_ref, w_ref, out_ref,
    behind, front_even, front_odd, side, corner, first, heads, send_sem, recv_sem,
):
    p, n = lax.axis_index("pts"), lax.axis_index("nbr")
    n_p, n_n = lax.axis_size("pts"), lax.axis_size("nbr")
    barrier = pltpu.get_barrier_semaphore()
    near = ((0, 1), (1, 0), (1, 1))
    up = [((p + dp) % n_p, (n + dn) % n_n) for dp, dn in near]
    down = [((p - dp + n_p) % n_p, (n - dn + n_n) % n_n) for dp, dn in near]
    for device in down:
        pl.semaphore_signal(barrier, inc=1, device_id=device, device_id_type=MESH)
    pl.semaphore_wait(barrier, 3)

    sent = [
        (0, even_ref.at[NX - 1, :, pl.ds(C, 2 * C)], front_even),
        (0, odd_ref.at[NX - 1, :, pl.ds(C, 2 * C)], front_odd),
        (1, last_ref, side),
        (2, last_ref.at[pl.ds(112, 16)], corner),
    ]
    copies = []
    for at, (way, source, target) in enumerate(sent):
        dp, dn = near[way]
        there = (p + dp < n_p) & (n + dn < n_n)
        here = (p - dp >= 0) & (n - dn >= 0)
        copy = pltpu.make_async_remote_copy(
            source, target, send_sem.at[at], recv_sem.at[at], device_id=up[way], device_id_type=MESH
        )
        copies.append((there, here, copy, target))

        @pl.when(there)
        def _():
            copy.start()

    taps = 3 * C
    for x in range(NX):
        line = odd_ref[x].astype(F32)
        behind[x] = jnp.concatenate([jnp.zeros((8, taps), F32), line[:120]], axis=0).astype(BF16)

    def held(x):
        return jnp.concatenate([behind[x], even_ref[x], odd_ref[x]], axis=1)

    for i in range(0, NX // 2, 2):
        lhs = [
            jnp.concatenate([held(2 * i + a - 1), held(2 * i + a + 1)], axis=0)
            for a in range(0 if i else 1, 3)
        ]
        weights = w_ref[...] if i else w_ref[3 * taps :, :]
        acc = jnp.dot(jnp.concatenate(lhs, axis=1), weights, preferred_element_type=F32)
        low, high = acc[:128], acc[128:]
        if i == 0:
            first[...] = low
            high = high + jnp.dot(held(1), w_ref[: 3 * taps, :], preferred_element_type=F32)
        else:
            heads[i] = low[:16]
            out_ref[i] = low.astype(BF16)
        heads[i + 1] = high[:16]
        out_ref[i + 1] = high.astype(BF16)

    for there, here, copy, target in copies:

        @pl.when(here)
        def _():
            copy.wait_recv()

        @pl.when(jnp.logical_not(here))
        def _():
            target[...] = jnp.zeros(target.shape, BF16)

    def widened(lines):
        lines = lines.astype(F32).reshape(-1, 8, 2 * C)
        odd = lines[:, :, C:]
        below = jnp.concatenate([jnp.zeros((odd.shape[0], 1, C), F32), odd[:, :7]], axis=1)
        return jnp.concatenate([below, lines], axis=2)

    edge = widened(side[...]).reshape(NX // 2, 2, 8, taps)
    before = widened(corner[...])[1:]
    lhs = jnp.concatenate(
        [jnp.concatenate([before, edge[: NX // 2 - 1, 1]], axis=0), edge[:, 0], edge[:, 1]], axis=2
    )
    beside_w = jnp.concatenate([w_ref[3 * a * taps : (3 * a + 1) * taps, :] for a in range(3)], axis=0)
    beside = jnp.dot(
        lhs.reshape(NX // 2 * 8, 3 * taps).astype(BF16), beside_w, preferred_element_type=F32
    )
    odd = widened(front_odd[...]).reshape(128, taps)
    lhs = jnp.concatenate(
        [
            jnp.concatenate([jnp.zeros((8, taps), F32), odd[:120]], axis=0),
            widened(front_even[...]).reshape(128, taps),
            odd,
        ],
        axis=1,
    )
    ahead = first[...] + jnp.dot(lhs.astype(BF16), w_ref[: 3 * taps, :], preferred_element_type=F32)
    out_ref[0] = ahead.astype(BF16)
    heads[0] = ahead[:16]
    for i in range(NX // 2):
        head = heads[i]
        head = jnp.concatenate([head[:8] + beside[8 * i : 8 * i + 8], head[8:]], axis=0)
        out_ref[i, 0:16, :] = head.astype(BF16)
    for there, here, copy, target in copies:

        @pl.when(there)
        def _():
            copy.wait_send()


def lower(even, odd, last, w_down):
    dma = pltpu.SemaphoreType.DMA
    return pl.pallas_call(
        lower_kernel,
        out_shape=jax.ShapeDtypeStruct((NX // 2, 128, 2 * C), BF16),
        in_specs=[VMEM, VMEM, VMEM, VMEM],
        out_specs=VMEM,
        scratch_shapes=[
            pltpu.VMEM((NX, 128, 3 * C), BF16),
            pltpu.VMEM((128, 2 * C), BF16),
            pltpu.VMEM((128, 2 * C), BF16),
            pltpu.VMEM((128, 2 * C), BF16),
            pltpu.VMEM((16, 2 * C), BF16),
            pltpu.VMEM((128, 2 * C), F32),
            pltpu.VMEM((NX // 2, 16, 2 * C), F32),
            dma((4,)),
            dma((4,)),
        ],
        compiler_params=pltpu.CompilerParams(
            collective_id=1, has_side_effects=True, vmem_limit_bytes=24 << 20
        ),
    )(even, odd, last, w_down)


def body(points, dest_owner, dest_cell, level_input, w_res, w_down):
    got, got_cells, base = exchange(
        dest_owner.reshape(1, ROWS), dest_cell.reshape(1, ROWS), points.reshape(ROWS, C), level_input, w_res
    )
    even, odd, last = scatter(
        got_cells.reshape(DEV * 2 * CAP), got.reshape(DEV * CAP, C), base.reshape(CELLS, C)
    )
    lowered = lower(even, odd, last, w_down.reshape(27 * C, 2 * C))
    return lowered.reshape(NX // 2, NY // 2, NZ // 2, 2 * C)


def solution(mesh):
    return jax.shard_map(
        body,
        mesh=mesh,
        in_specs=(
            P("pts", "nbr", None, None),
            P("pts", "nbr", None, None),
            P("pts", "nbr", None),
            P("nbr", "pts", None, None),
            P(),
            P(),
        ),
        out_specs=P("nbr", "pts", None, None),
        check_vma=False,
    )
```

```python
import functools

import jax
import jax.numpy as jnp
from jax import lax
from jax.experimental import pallas as pl
from jax.experimental.pallas import tpu as pltpu
from jax.sharding import PartitionSpec as P

MESH = pl.DeviceIdType.MESH
F32, BF16, I32 = jnp.float32, jnp.bfloat16, jnp.int32
DEV, CAP, ROWS, C = 128, 64, 4096, 128
NX, NY, NZ = 16, 32, 16
CELLS = NX * NY * NZ
CHAINS = 8
LAYERS = 4
VMEM = pl.BlockSpec(memory_space=pltpu.VMEM)
SMEM = pl.BlockSpec(memory_space=pltpu.SMEM)
ANY = pl.BlockSpec(memory_space=pl.ANY)
HBM = pl.BlockSpec(memory_space=pltpu.HBM)


def find_slots(own_ref, cell_ref, hit_ref, val_ref, idx_ref, cells_ref):
    block = 256
    hit_ref[...] = (lax.broadcasted_iota(I32, (DEV, ROWS), 0) == own_ref[...]).astype(F32).astype(BF16)
    before = (
        lax.broadcasted_iota(I32, (block, block), 0) < lax.broadcasted_iota(I32, (block, block), 1)
    ).astype(F32).astype(BF16)
    carry = jnp.zeros((DEV, 1), F32)
    for b in range(ROWS // block):
        span = slice(b * block, (b + 1) * block)
        hit = hit_ref[:, span]
        hit32 = hit.astype(F32)
        ranks = jnp.dot(hit, before, preferred_element_type=F32) + carry
        rank = jnp.sum(ranks * hit32, axis=0, keepdims=True).astype(I32)
        carry = carry + jnp.sum(hit32, axis=1, keepdims=True)
        place = lax.broadcasted_iota(I32, (CAP, block), 0) == rank
        row = lax.broadcasted_iota(I32, (1, block), 1) + b * block + 8
        cell = cell_ref[:, span]
        for part, value in enumerate((row % 64, row // 64, cell % 64, cell // 64)):
            chosen = jnp.where(place, value.astype(F32), 0.0)
            val_ref[part * CAP : (part + 1) * CAP, span] = chosen.astype(BF16)
    found = lax.dot_general(
        hit_ref[...], val_ref[...], (((1,), (1,)), ((), ())), preferred_element_type=F32
    ).astype(I32)
    idx_ref[:, :CAP] = jnp.clip(found[:, CAP : 2 * CAP] * 64 + found[:, :CAP], 0, ROWS + 7)
    idx_ref[:, CAP:] = jnp.zeros((DEV, CAP), I32)
    cells = found[:, 3 * CAP :] * 64 + found[:, 2 * CAP : 3 * CAP]
    full = found[:, CAP : 2 * CAP] + found[:, :CAP] > 0
    cells = jnp.where(full, cells, lax.broadcasted_iota(I32, (DEV, CAP), 1) * NZ)
    cells_ref[...] = jnp.concatenate([cells, jnp.zeros((DEV, CAP), I32)], axis=1).reshape(DEV, 1, 2 * CAP)


def partner(k, p, n):
    t = (k * 37) % DEV
    dx, dz, dy, dc = t % 4, (t // 4) % 4, (t // 16) % 4, t // 64
    return (p // 4 + dx) % 4 * 4 + (p % 4 + dz) % 4, (n // 2 + dy) % 4 * 2 + (n % 2 + dc) % 2


def exchange_kernel(
    own_hbm, cell_hbm, pts_hbm, level_ref, w_hbm,
    got_ref, got_cells_ref, base,
    owner_of, cell_of, hit, val, idx_vmem, idx_ref, cells_ref, pts, taps, rows32, packed, ext, s0, s1, s2, wide,
    row_send, row_recv, cell_send, cell_recv, own_sem, own_cell_sem, in_sem, pts_sem, taps_sem, list_sem, halo_send, halo_recv,
):
    p, n = lax.axis_index("pts"), lax.axis_index("nbr")
    n_p, n_n = lax.axis_size("pts"), lax.axis_size("nbr")
    me = p * n_n + n
    barrier = pltpu.get_barrier_semaphore()
    lists_in = [
        pltpu.make_async_copy(own_hbm, owner_of, list_sem.at[0]),
        pltpu.make_async_copy(cell_hbm, cell_of, list_sem.at[1]),
    ]
    pts_in = pltpu.make_async_copy(pts_hbm, pts, pts_sem)
    for copy in lists_in:
        copy.start()
    pts_in.start()

    def greet(k, carry):
        for d in range(n_n):
            device = ((p + k) % n_p, (n + d) % n_n)
            pl.semaphore_signal(barrier, inc=1, device_id=device, device_id_type=MESH)
        return carry

    for d in range(1, n_n):
        pl.semaphore_signal(barrier, inc=1, device_id=(p, (n + d) % n_n), device_id_type=MESH)
    lax.fori_loop(1, n_p, greet, 0)
    inner = pltpu.make_async_copy(level_ref, ext.at[pl.ds(1, NX), pl.ds(1, NY)], in_sem)
    inner.start()
    taps_in = pltpu.make_async_copy(w_hbm, taps, taps_sem)
    taps_in.start()
    for copy in lists_in:
        copy.wait()
    find_slots(owner_of, cell_of, hit, val, idx_vmem, cells_ref)
    idx_in = pltpu.make_async_copy(idx_vmem, idx_ref, list_sem.at[2])
    idx_in.start()
    rows32[:8, :] = jnp.zeros((8, C), F32)
    pts_in.wait()
    rows32[8:, :] = pts[...].astype(F32)
    idx_in.wait()

    def gather(owner):
        for g in range(CAP // 16):
            rows = [rows32[pl.ds(idx_ref[owner, g * 16 + r], 1), :] for r in range(16)]
            packed[owner, g * 16 : (g + 1) * 16, :] = jnp.concatenate(rows, axis=0).astype(BF16)

    gather(me)
    own = pltpu.make_async_copy(packed.at[me], got_ref.at[me], own_sem)
    own.start()
    own_cells = pltpu.make_async_copy(cells_ref.at[me], got_cells_ref.at[me], own_cell_sem)
    own_cells.start()
    pl.semaphore_wait(barrier, DEV - 1)

    sides = []
    for dn in (-1, 0, 1):
        for dp in (-1, 0, 1):
            if dn == 0 and dp == 0:
                continue
            sx = pl.ds(0, NX) if dn == 0 else pl.ds(NX - 1 if dn > 0 else 0, 1)
            sy = pl.ds(0, NY) if dp == 0 else pl.ds(NY - 1 if dp > 0 else 0, 1)
            tx = pl.ds(1, NX) if dn == 0 else pl.ds(0 if dn > 0 else NX + 1, 1)
            ty = pl.ds(1, NY) if dp == 0 else pl.ds(0 if dp > 0 else NY + 1, 1)
            at = len(sides)
            to_n, to_p, from_n, from_p = n + dn, p + dp, n - dn, p - dp
            there = (to_n >= 0) & (to_n < n_n) & (to_p >= 0) & (to_p < n_p)
            here = (from_n >= 0) & (from_n < n_n) & (from_p >= 0) & (from_p < n_p)
            copy = pltpu.make_async_remote_copy(
                level_ref.at[sx, sy], ext.at[tx, ty], halo_send.at[at], halo_recv.at[at],
                device_id=((p + dp + n_p) % n_p, (n + dn + n_n) % n_n), device_id_type=MESH,
            )
            sides.append((there, here, copy, tx, ty))

            @pl.when(there)
            def _():
                copy.start()

    def send(k, carry):
        tp, tn = partner(k, p, n)
        owner = tp * n_n + tn
        gather(owner)
        pltpu.make_async_remote_copy(
            packed.at[owner], got_ref.at[me], row_send, row_recv, device_id=(tp, tn), device_id_type=MESH
        ).start()
        pltpu.make_async_remote_copy(
            cells_ref.at[owner], got_cells_ref.at[me], cell_send, cell_recv,
            device_id=(tp, tn), device_id_type=MESH,
        ).start()
        return carry

    lax.fori_loop(1, DEV, send, 0)

    taps_in.wait()
    for a in range(3):
        for q in range(2):
            for c in range(3):
                for pin in range(2):
                    for pout in range(2):
                        b = 2 * q + pin - pout
                        at = (a * 2 + q) * 3 + c
                        tap = taps[9 * a + 3 * b + c] if 0 <= b <= 2 else jnp.zeros((C, C), BF16)
                        wide[at * 256 + pin * C : at * 256 + (pin + 1) * C, pout * C : (pout + 1) * C] = tap

    inner.wait()
    for there, here, copy, tx, ty in sides:
        shape = (tx.size, ty.size, NZ, C)

        @pl.when(here)
        def _():
            copy.wait_recv()

        @pl.when(jnp.logical_not(here))
        def _():
            ext[tx, ty] = jnp.zeros(shape, BF16)

    def shift(x, carry):
        for q in range(NY // 2 + 1):
            for part in range(2):
                line = ext[x, 2 * q + part]
                line32 = line.astype(F32)
                edge = jnp.zeros((1, C), F32)
                lanes = slice(part * C, (part + 1) * C)
                s1[x, q, :, lanes] = line
                s0[x, q, :, lanes] = jnp.concatenate([edge, line32[: NZ - 1]], axis=0).astype(BF16)
                s2[x, q, :, lanes] = jnp.concatenate([line32[1:], edge], axis=0).astype(BF16)
        return carry

    lax.fori_loop(0, NX + 2, shift, 0)

    half = NY // 2

    def conv(t, carry):
        i = t * LAYERS
        lhs = jnp.concatenate(
            [
                s[pl.ds(i + a, LAYERS), q : q + half].reshape(LAYERS * half * NZ, 2 * C)
                for a in range(3)
                for q in range(2)
                for s in (s0, s1, s2)
            ],
            axis=1,
        )
        both = jnp.maximum(jnp.dot(lhs, wide[...], preferred_element_type=F32), 0.0)
        low = s1[pl.ds(i + 1, LAYERS), :half, :, C:].astype(F32)
        high = s1[pl.ds(i + 1, LAYERS), 1:, :, :C].astype(F32)
        base[pl.ds(i, LAYERS), :, 0] = both[:, :C].reshape(LAYERS, half, NZ, C) + low
        base[pl.ds(i, LAYERS), :, 1] = both[:, C:].reshape(LAYERS, half, NZ, C) + high
        return carry

    lax.fori_loop(0, NX // LAYERS, conv, 0)

    own.wait()
    own_cells.wait()
    for there, here, copy, tx, ty in sides:

        @pl.when(there)
        def _():
            copy.wait_send()

    most = pl.ds(0, DEV - 1)
    pltpu.make_async_copy(packed.at[most], got_ref.at[most], row_send).wait()
    pltpu.make_async_copy(cells_ref.at[most], got_cells_ref.at[most], cell_send).wait()
    pltpu.make_async_copy(packed.at[most], got_ref.at[most], row_recv).wait()
    pltpu.make_async_copy(cells_ref.at[most], got_cells_ref.at[most], cell_recv).wait()


def exchange(own, cell, pts, level, w_res):
    dma = pltpu.SemaphoreType.DMA
    padded = (NX + 2, NY // 2 + 1, NZ, 2 * C)
    return pl.pallas_call(
        exchange_kernel,
        out_shape=(
            jax.ShapeDtypeStruct((DEV, CAP, C), BF16),
            jax.ShapeDtypeStruct((DEV, 1, 2 * CAP), I32),
            jax.ShapeDtypeStruct((NX, NY // 2, 2, NZ, C), F32),
        ),
        in_specs=[HBM, HBM, HBM, HBM, HBM],
        out_specs=(VMEM, VMEM, VMEM),
        scratch_shapes=[
            pltpu.VMEM((1, ROWS), I32),
            pltpu.VMEM((1, ROWS), I32),
            pltpu.VMEM((DEV, ROWS), BF16),
            pltpu.VMEM((4 * CAP, ROWS), BF16),
            pltpu.VMEM((DEV, 2 * CAP), I32),
            pltpu.SMEM((DEV, 2 * CAP), I32),
            pltpu.VMEM((DEV, 1, 2 * CAP), I32),
            pltpu.VMEM((ROWS, C), BF16),
            pltpu.VMEM((27, C, C), BF16),
            pltpu.VMEM((ROWS + 8, C), F32),
            pltpu.VMEM((DEV, CAP, C), BF16),
            pltpu.VMEM((NX + 2, NY + 2, NZ, C), BF16),
            pltpu.VMEM(padded, BF16),
            pltpu.VMEM(padded, BF16),
            pltpu.VMEM(padded, BF16),
            pltpu.VMEM((18 * 256, 256), BF16),
            dma, dma, dma, dma, dma, dma, dma, dma, dma, dma((3,)), dma((8,)), dma((8,)),
        ],
        compiler_params=pltpu.CompilerParams(
            collective_id=0, has_side_effects=True, vmem_limit_bytes=36 << 20
        ),
    )(*(pltpu.with_memory_space_constraint(x, pltpu.HBM) for x in (own, cell, pts, level, w_res)))


def scatter_kernel(cells_in, got_ref, base_ref, even_ref, odd_ref, last_ref, cells_ref, sem, rows32, *sums):
    listed = pltpu.make_async_copy(cells_in, cells_ref, sem)
    listed.start()

    def clear(t, carry):
        span = pl.ds(pl.multiple_of(t * 32, 32), 32)
        for total in sums:
            total[span, :] = jnp.zeros((32, C), F32)
        rows32[span, :] = got_ref[span, :].astype(F32)
        return carry

    lax.fori_loop(0, CELLS // 32, clear, 0)
    share = DEV // CHAINS
    listed.wait()

    def add(s, carry):
        for g in range(CAP // 16):
            for r in range(g * 16, g * 16 + 16):
                at = [cells_ref[(k * share + s) * (2 * CAP) + r] for k in range(CHAINS)]
                new = [
                    sums[k][pl.ds(at[k], 1), :] + rows32[pl.ds((k * share + s) * CAP + r, 1), :]
                    for k in range(CHAINS)
                ]
                for k in range(CHAINS):
                    sums[k][pl.ds(at[k], 1), :] = new[k]
        return carry

    lax.fori_loop(0, share, add, 0)

    def deal(x, carry):
        top = lax.broadcasted_iota(I32, (NZ // 2, C), 0) == 0

        def total(y, start):
            at = pl.ds((x * NY + y) * NZ + start, NZ // 2, stride=2)
            value = base_ref[at, :]
            for more in sums:
                value = value + more[at, :]
            return value

        for parity, out_ref in ((0, even_ref), (1, odd_ref)):
            for j in range(0, NY // 2, 2):
                parts = []
                for y in (2 * j + parity, 2 * j + 2 + parity):
                    even, odd = total(y, 0), total(y, 1)
                    below = jnp.where(top, 0.0, pltpu.roll(odd, 1, 0))
                    parts.append((below, even, odd))
                for c in range(3):
                    pair = jnp.concatenate([parts[0][c], parts[1][c]], axis=0).astype(BF16)
                    out_ref[x, j * 8 : j * 8 + 16, c * C : (c + 1) * C] = pair
        return carry

    lax.fori_loop(0, NX, deal, 0)
    for x in range(0, NX, 2):
        parts = [odd_ref[x + h, 112:128, C:].astype(F32)[8:] for h in range(2)]
        last_ref[x * 8 : x * 8 + 16, :] = jnp.concatenate(parts, axis=0).astype(BF16)


def scatter(cells, got, base):
    return pl.pallas_call(
        scatter_kernel,
        out_shape=(
            jax.ShapeDtypeStruct((NX, 128, 3 * C), BF16),
            jax.ShapeDtypeStruct((NX, 128, 3 * C), BF16),
            jax.ShapeDtypeStruct((128, 2 * C), BF16),
        ),
        in_specs=[ANY, VMEM, VMEM],
        out_specs=(VMEM, VMEM, VMEM),
        scratch_shapes=[pltpu.SMEM((DEV * 2 * CAP,), I32), pltpu.SemaphoreType.DMA]
        + [pltpu.VMEM((CELLS, C), F32)] * (1 + CHAINS),
        compiler_params=pltpu.CompilerParams(vmem_limit_bytes=40 << 20),
    )(cells, got, base)


def lower_kernel(
    even_ref, odd_ref, last_ref, w_ref, out_ref,
    behind, front_even, front_odd, side, corner, first, heads, send_sem, recv_sem,
):
    p, n = lax.axis_index("pts"), lax.axis_index("nbr")
    n_p, n_n = lax.axis_size("pts"), lax.axis_size("nbr")
    barrier = pltpu.get_barrier_semaphore()
    near = ((0, 1), (1, 0), (1, 1))
    up = [((p + dp) % n_p, (n + dn) % n_n) for dp, dn in near]
    down = [((p - dp + n_p) % n_p, (n - dn + n_n) % n_n) for dp, dn in near]
    for device in down:
        pl.semaphore_signal(barrier, inc=1, device_id=device, device_id_type=MESH)
    pl.semaphore_wait(barrier, 3)

    sent = [
        (0, even_ref.at[NX - 1, :, pl.ds(C, 2 * C)], front_even),
        (0, odd_ref.at[NX - 1, :, pl.ds(C, 2 * C)], front_odd),
        (1, last_ref, side),
        (2, last_ref.at[pl.ds(112, 16)], corner),
    ]
    copies = []
    for at, (way, source, target) in enumerate(sent):
        dp, dn = near[way]
        there = (p + dp < n_p) & (n + dn < n_n)
        here = (p - dp >= 0) & (n - dn >= 0)
        copy = pltpu.make_async_remote_copy(
            source, target, send_sem.at[at], recv_sem.at[at], device_id=up[way], device_id_type=MESH
        )
        copies.append((there, here, copy, target))

        @pl.when(there)
        def _():
            copy.start()

    taps = 3 * C
    for x in range(NX):
        line = odd_ref[x].astype(F32)
        behind[x] = jnp.concatenate([jnp.zeros((8, taps), F32), line[:120]], axis=0).astype(BF16)

    def held(x):
        return jnp.concatenate([behind[x], even_ref[x], odd_ref[x]], axis=1)

    for i in range(0, NX // 2, 2):
        lhs = [
            jnp.concatenate([held(2 * i + a - 1), held(2 * i + a + 1)], axis=0)
            for a in range(0 if i else 1, 3)
        ]
        weights = w_ref[...] if i else w_ref[3 * taps :, :]
        acc = jnp.dot(jnp.concatenate(lhs, axis=1), weights, preferred_element_type=F32)
        low, high = acc[:128], acc[128:]
        if i == 0:
            first[...] = low
            high = high + jnp.dot(held(1), w_ref[: 3 * taps, :], preferred_element_type=F32)
        else:
            heads[i] = low[:16]
            out_ref[i] = low.astype(BF16)
        heads[i + 1] = high[:16]
        out_ref[i + 1] = high.astype(BF16)

    for there, here, copy, target in copies:

        @pl.when(here)
        def _():
            copy.wait_recv()

        @pl.when(jnp.logical_not(here))
        def _():
            target[...] = jnp.zeros(target.shape, BF16)

    def widened(lines):
        lines = lines.astype(F32).reshape(-1, 8, 2 * C)
        odd = lines[:, :, C:]
        below = jnp.concatenate([jnp.zeros((odd.shape[0], 1, C), F32), odd[:, :7]], axis=1)
        return jnp.concatenate([below, lines], axis=2)

    edge = widened(side[...]).reshape(NX // 2, 2, 8, taps)
    before = widened(corner[...])[1:]
    lhs = jnp.concatenate(
        [jnp.concatenate([before, edge[: NX // 2 - 1, 1]], axis=0), edge[:, 0], edge[:, 1]], axis=2
    )
    beside_w = jnp.concatenate([w_ref[3 * a * taps : (3 * a + 1) * taps, :] for a in range(3)], axis=0)
    beside = jnp.dot(
        lhs.reshape(NX // 2 * 8, 3 * taps).astype(BF16), beside_w, preferred_element_type=F32
    )
    odd = widened(front_odd[...]).reshape(128, taps)
    lhs = jnp.concatenate(
        [
            jnp.concatenate([jnp.zeros((8, taps), F32), odd[:120]], axis=0),
            widened(front_even[...]).reshape(128, taps),
            odd,
        ],
        axis=1,
    )
    ahead = first[...] + jnp.dot(lhs.astype(BF16), w_ref[: 3 * taps, :], preferred_element_type=F32)
    out_ref[0] = ahead.astype(BF16)
    heads[0] = ahead[:16]
    for i in range(NX // 2):
        head = heads[i]
        head = jnp.concatenate([head[:8] + beside[8 * i : 8 * i + 8], head[8:]], axis=0)
        out_ref[i, 0:16, :] = head.astype(BF16)
    for there, here, copy, target in copies:

        @pl.when(there)
        def _():
            copy.wait_send()


def lower(even, odd, last, w_down):
    dma = pltpu.SemaphoreType.DMA
    return pl.pallas_call(
        lower_kernel,
        out_shape=jax.ShapeDtypeStruct((NX // 2, 128, 2 * C), BF16),
        in_specs=[VMEM, VMEM, VMEM, VMEM],
        out_specs=VMEM,
        scratch_shapes=[
            pltpu.VMEM((NX, 128, 3 * C), BF16),
            pltpu.VMEM((128, 2 * C), BF16),
            pltpu.VMEM((128, 2 * C), BF16),
            pltpu.VMEM((128, 2 * C), BF16),
            pltpu.VMEM((16, 2 * C), BF16),
            pltpu.VMEM((128, 2 * C), F32),
            pltpu.VMEM((NX // 2, 16, 2 * C), F32),
            dma((4,)),
            dma((4,)),
        ],
        compiler_params=pltpu.CompilerParams(
            collective_id=1, has_side_effects=True, vmem_limit_bytes=24 << 20
        ),
    )(even, odd, last, w_down)


def body(points, dest_owner, dest_cell, level_input, w_res, w_down):
    got, got_cells, base = exchange(
        dest_owner.reshape(1, ROWS), dest_cell.reshape(1, ROWS), points.reshape(ROWS, C), level_input, w_res
    )
    even, odd, last = scatter(
        got_cells.reshape(DEV * 2 * CAP), got.reshape(DEV * CAP, C), base.reshape(CELLS, C)
    )
    lowered = lower(even, odd, last, w_down.reshape(27 * C, 2 * C))
    return lowered.reshape(NX // 2, NY // 2, NZ // 2, 2 * C)


def solution(mesh):
    return jax.shard_map(
        body,
        mesh=mesh,
        in_specs=(
            P("pts", "nbr", None, None),
            P("pts", "nbr", None, None),
            P("pts", "nbr", None),
            P("nbr", "pts", None, None),
            P(),
            P(),
        ),
        out_specs=P("nbr", "pts", None, None),
        check_vma=False,
    )
```
